32 devices in a mesh: band: 2 (over y), rtile: 4 (over z), stile: 2 (over x), freq: 2 (over core).
Axes of the slice: x: 2, y: 2, z: 4, core: 2. Of those that a mesh axis runs over, the one named last changes fastest.
Arguments:
- x_start: float32 [4, 8, 2, 256, 128], P(('band', 'freq'), 'rtile', None, None, 'stile'), parts along dimension 0, may hold values from -6 to 6
- data: float32 [4, 4, 2, 2, 256, 128], P(('band', 'freq'), 'rtile', 'stile'), parts along dimension 0, may hold values from -6 to 6
- u_fac: bfloat16 [4, 4, 2, 8, 2, 64, 256], P(('band', 'freq'), 'rtile', 'stile'), parts along dimension 0, may hold values from -0.75 to 0.75
- v_fac: bfloat16 [4, 4, 2, 8, 2, 64, 256], P(('band', 'freq'), None, 'stile', 'rtile'), parts along dimension 0, may hold values from -0.125 to 0.125
- ranks: int32 [4, 4, 2, 8], P(('band', 'freq'), None, 'stile'), parts along dimension 0, may hold values from 8 to 56, as said below
- slot_tile: int32 [8], replicated, may hold values from 0 to 7, as said below
- neighbours: int32 [8, 4], replicated, may hold values from -1 to 7, as said below
Outputs:
- x_final: float32 [4, 8, 2, 256, 128], P(('band', 'freq'), 'rtile', None, None, 'stile'), parts along dimension 0
- z_final: float32 [4, 8, 2, 256, 128], P(('band', 'freq'), 'rtile', None, None, 'stile'), parts along dimension 0
The draws below stay inside these ranges and needn't reach their ends.
There are 2 independent parts, one for each index of `band`. The reference program is written for one: setup_inputs(seed, part) draws one part's arguments, and reference() takes and returns one part's arrays. A program takes and returns all parts, laid end to end along the dimension named above; an argument that names none is the same for every part. Nothing has to cross between parts.
Inputs may be any that keep to these rules, and one draw needn't show every extreme that they name: Each entry is a whole multiple of one eighth of 64; for every frequency and source tile the ranks of tiles 2k and 2k+1 sum to at most 64, and for at least one frequency and source tile they sum to exactly 64. `slot_tile`: each tile appears in exactly one slot; slots 2p and 2p+1 hold the two tiles 2k and 2k+1 of one k. `neighbours`: tiles lie on a grid of four tiles a row, tile t in row t // 4; an entry is -1 or the adjacent tile in that direction, and the lists are symmetric (if tile s is east of t, t is west of s; likewise south and north).
All inputs are finite; a program needn't handle non-finite values.
Results may differ from the reference program's by a relative error of at most 0.0024.
Values may be sent and summed in bfloat16 or wider, within the bound.
A program may use at most 64 MiB of HBM per device.

```python
import jax
import jax.numpy as jnp
from jax import lax

EDGE = 16
TILE = 256
RANK = 64
VS = 128
ITERS = 2
NRT = 8
NSR = 4
NSC = 2
FREQS = 2
RECEIVERS = 2048


def draw_ranks(key, part):
    key = jax.random.fold_in(key, 11)
    key_one, key_two, key_three = jax.random.split(key, 3)
    shape = (FREQS, NSR, NSC, NRT // 2)
    first = jax.random.randint(key_one, shape, 1, 8)
    second = jax.random.randint(key_two, shape, 1, 9 - first)
    first = first.at[0, 0, 0, 0].set(7)
    second = second.at[0, 0, 0, 0].set(1)
    flip = jax.random.randint(key_three, shape, 0, 2)
    lower = jnp.where(flip == 1, second, first)
    upper = jnp.where(flip == 1, first, second)
    levels = jnp.stack([lower, upper], axis=-1).reshape(FREQS, NSR, NSC, NRT)
    return (levels * (RANK // 8)).astype(jnp.int32)


def draw_slot_tile(key, part):
    key = jax.random.fold_in(key, 31)
    key_order, key_flip = jax.random.split(key)
    order = jax.random.permutation(key_order, NRT // 2).astype(jnp.int32)
    flip = jax.random.randint(key_flip, (NRT // 2,), 0, 2).astype(jnp.int32)
    first = 2 * order + flip
    second = 2 * order + 1 - flip
    return jnp.stack([first, second], axis=1).reshape(NRT).astype(jnp.int32)


def draw_neighbours(key, part):
    key = jax.random.fold_in(key, 23)
    key_east, key_south = jax.random.split(key)
    index = jnp.arange(NRT, dtype=jnp.int32)
    east_link = (jax.random.randint(key_east, (NRT,), 0, 4) > 0) & (index % 4 < 3)
    east_link = east_link.at[NRT - 2].set(True)
    south_link = (jax.random.randint(key_south, (NRT,), 0, 4) > 0) & (index < NRT - 4)
    west_link = jnp.roll(east_link, 1) & (index % 4 > 0)
    north_link = jnp.roll(south_link, 4) & (index >= 4)
    eastward = jnp.where(east_link, index + 1, -1)
    southward = jnp.where(south_link, index + 4, -1)
    westward = jnp.where(west_link, index - 1, -1)
    northward = jnp.where(north_link, index - 4, -1)
    return jnp.stack([eastward, southward, westward, northward], axis=1).astype(jnp.int32)


def steps_of(key, dims, shards, smallest, top_value):
    factor_of, own = 1.0, jax.random.fold_in(key, 6)
    for axis_at, shards_of in shards:
        steps = jnp.exp(jax.random.uniform(jax.random.fold_in(own, axis_at), (shards_of,), jnp.float32, smallest / len(shards), top_value / len(shards)))
        factor_of = factor_of * jnp.repeat(steps, dims[axis_at] // shards_of).reshape([-1 if axis == axis_at else 1 for axis in range(len(dims))])
    return factor_of


def scatter_about(own_key, extent, width, bound, cuts=(), kind=jnp.bfloat16):
    factor_of = steps_of(own_key, extent, cuts, -0.22, 0.18) if cuts else 1.0
    values = jax.random.normal(own_key, extent, jnp.float32) * width * factor_of
    return jnp.minimum(jnp.maximum(values, -bound), bound).astype(kind)


def setup_inputs(seed: int = 0, part: int = 0) -> dict:
    streams_of = jax.random.split(jax.random.key(seed), 8)
    part_splits = jax.random.split(jax.random.fold_in(streams_of[7], part), 8)
    return {
        "x_start": scatter_about(part_splits[0], (FREQS, NRT, 2, TILE, VS), 1.0, 6.0, ((0, 2), (1, 4), (4, 2)), jnp.float32),
        "data": scatter_about(part_splits[1], (FREQS, NSR, NSC, 2, TILE, VS), 1.0, 6.0, ((0, 2), (1, 4), (2, 2)), jnp.float32),
        "u_fac": scatter_about(part_splits[2], (FREQS, NSR, NSC, NRT, 2, RANK, TILE), RANK ** -0.5, 0.75, ((0, 2), (1, 4), (2, 2))),
        "v_fac": scatter_about(part_splits[3], (FREQS, NSR, NSC, NRT, 2, RANK, TILE), RECEIVERS ** -0.5, 0.125, ((0, 2), (2, 2), (3, 4))),
        "ranks": draw_ranks(jax.random.fold_in(jax.random.fold_in(streams_of[7], part), 71), part),
        "slot_tile": draw_slot_tile(jax.random.fold_in(streams_of[7], 71), part),
        "neighbours": draw_neighbours(jax.random.fold_in(streams_of[7], 71), part),
    }


def conj_apply(factor, field, form):
    fa = factor[..., 0, :, :].astype(jnp.float32)
    fb = factor[..., 1, :, :].astype(jnp.float32)
    xa = field[..., 0, :, :].astype(jnp.float32)
    xb = field[..., 1, :, :].astype(jnp.float32)
    real = jnp.einsum(form, fa, xa) + jnp.einsum(form, fb, xb)
    imag = jnp.einsum(form, fa, xb) - jnp.einsum(form, fb, xa)
    return jnp.stack([real, imag], axis=-3)

def plain_apply(factor, panel, form):
    fa = factor[..., 0, :, :].astype(jnp.float32)
    fb = factor[..., 1, :, :].astype(jnp.float32)
    pa = panel[..., 0, :, :].astype(jnp.float32)
    pb = panel[..., 1, :, :].astype(jnp.float32)
    real = jnp.einsum(form, fa, pa) - jnp.einsum(form, fb, pb)
    imag = jnp.einsum(form, fa, pb) + jnp.einsum(form, fb, pa)
    return jnp.stack([real, imag], axis=-3)

def interior(grid):
    diff_a = grid[:, :, 1:] - grid[:, :, :-1]
    diff_b = grid[:, :, :, 1:] - grid[:, :, :, :-1]
    zero_pad = [(0, 0)] * 5
    after_a = list(zero_pad)
    after_a[2] = (0, 1)
    before_a = list(zero_pad)
    before_a[2] = (1, 0)
    after_b = list(zero_pad)
    after_b[3] = (0, 1)
    before_b = list(zero_pad)
    before_b[3] = (1, 0)
    return jnp.pad(diff_a, after_a) - jnp.pad(diff_a, before_a) + jnp.pad(diff_b, after_b) - jnp.pad(diff_b, before_b)

def smoothing(field, present, source_slot):
    slots, parts, cells, columns = field.shape
    grid = field.reshape(slots, parts, EDGE, EDGE, columns)
    edges = jnp.stack([grid[:, :, :, EDGE - 1, :], grid[:, :, EDGE - 1, :, :], grid[:, :, :, 0, :], grid[:, :, 0, :, :]], axis=1)
    opposite = jnp.array([2, 3, 0, 1], dtype=jnp.int32)
    ghost = edges[source_slot, opposite[None, :]] * present[:, :, None, None, None]
    lap = interior(grid)
    lap = lap.at[:, :, :, EDGE - 1, :].add(present[:, 0, None, None, None] * (ghost[:, 0] - grid[:, :, :, EDGE - 1, :]))
    lap = lap.at[:, :, EDGE - 1, :, :].add(present[:, 1, None, None, None] * (ghost[:, 1] - grid[:, :, EDGE - 1, :, :]))
    lap = lap.at[:, :, :, 0, :].add(present[:, 2, None, None, None] * (ghost[:, 2] - grid[:, :, :, 0, :]))
    lap = lap.at[:, :, 0, :, :].add(present[:, 3, None, None, None] * (ghost[:, 3] - grid[:, :, 0, :, :]))
    return lap.reshape(field.shape)

def reference(x_start, data, u_fac, v_fac, ranks, slot_tile, neighbours):
    count = slot_tile.shape[0]
    inverse = jnp.zeros((count,), jnp.int32).at[slot_tile].set(jnp.arange(count, dtype=jnp.int32))
    listed = neighbours[slot_tile]
    present = (listed >= 0).astype(jnp.float32)
    source_slot = inverse[jnp.maximum(listed, 0)]

    def one_frequency(inputs):
        field, record, ufac, vfac, rank_tab = inputs
        x_now = field
        z_now = field
        u_now = jnp.zeros_like(field)
        for step in range(ITERS):
            rounded = x_now.astype(jnp.bfloat16)

            def row(total, pieces):
                rec_row, u_row, v_row, rank_row = pieces
                level = lax.broadcasted_iota(jnp.int32, rank_row.shape + (RANK,), 2)
                kept_tile = (level < rank_row[:, :, None]).astype(jnp.float32)
                kept_slot = kept_tile[:, slot_tile]
                panel = conj_apply(v_row, rounded, 'sqrt,qtv->sqrv').astype(jnp.bfloat16)
                panel = panel * kept_slot[:, :, None, :, None].astype(jnp.bfloat16)
                image = plain_apply(u_row[:, slot_tile], panel, 'sqrt,sqrv->stv')
                misfit = image - rec_row
                back = conj_apply(u_row, misfit.astype(jnp.bfloat16), 'sjrt,stv->sjrv')
                back = (back * kept_tile[:, :, None, :, None]).astype(jnp.bfloat16)
                return (total + plain_apply(v_row, back[:, slot_tile], 'sqrt,sqrv->qtv'), None)
            grad_data, unused = lax.scan(row, jnp.zeros(field.shape, jnp.float32), (record, ufac, vfac, rank_tab))
            lap = smoothing(x_now, present, source_slot)
            x_now = x_now - 0.1 * (grad_data - 0.25 * lap + 1.0 * (x_now - z_now + u_now))
            summed = x_now + u_now
            modulus = jnp.sqrt(summed[:, 0:1] ** 2 + summed[:, 1:2] ** 2)
            z_now = summed * (1.0 - 0.5 / jnp.maximum(modulus, 0.5))
            u_now = summed - z_now
        return (x_now, z_now)
    x_final, z_final = lax.map(one_frequency, (x_start, data, u_fac, v_fac, ranks))
    return (x_final, z_final)
```

```python
import functools

import jax
import jax.numpy as jnp
from jax import lax
from jax.experimental import pallas as pl
from jax.experimental.pallas import tpu as pltpu
from jax.sharding import PartitionSpec as P

EDGE = 16
ITERS = 2
F32 = jnp.float32
BF16 = jnp.bfloat16
MESH = pl.DeviceIdType.MESH


def dot(a, b):
    return lax.dot_general(a, b, (((1,), (0,)), ((), ())), preferred_element_type=F32)


def dot_t(a, b):
    return lax.dot_general(a, b, (((0,), (0,)), ((), ())), preferred_element_type=F32)


def swap(v):
    w = v.shape[1] // 2
    if v.shape[1] == 128:
        return pltpu.roll(v, w, 1)
    return jnp.concatenate([v[:, w:], v[:, :w]], axis=1)


def shift(v, by):
    n = v.shape[0]
    return pltpu.roll(v, by % n, 0)


def kernel(
    R, S,
    x_ref, d_ref, u_ref, v_ref, rk_ref, st_ref, nb_ref,
    xo_ref, zo_ref,
    vp, mk, up, dl, xs, zs, us,
    pan_out, pan_in, back_out, back_in, edge_out, edge_in0, edge_in1,
    v_send, v_recv, m_send, m_recv, p_send, p_recv, b_send, b_recv, e_send, e_recv,
):
    me_i = lax.axis_index("rtile")
    me_c = lax.axis_index("stile")
    rank = v_ref.shape[-2]
    tile = v_ref.shape[-1]
    w = x_ref.shape[-1]
    w2 = 2 * w
    count = st_ref.shape[0]
    blk = rank // 8

    barrier = pltpu.get_barrier_semaphore()
    for d in range(S):
        for k in range(R):
            if d or k:
                pl.semaphore_signal(
                    barrier, inc=1,
                    device_id={"rtile": lax.rem(me_i + k, R), "stile": lax.rem(me_c + d, S)},
                    device_id_type=MESH,
                )

    row = lax.broadcasted_iota(jnp.int32, (rank, tile), 0)

    def packed(a, b, ra, rb):
        a = a.astype(F32)
        b = b.astype(F32)
        b = jnp.concatenate([b[j * blk:(j + 1) * blk] for j in reversed(range(8))], axis=0)
        return jnp.where(row < ra, a, jnp.where(row >= rank - rb, b, 0.0)).astype(BF16)

    level = lax.broadcasted_iota(jnp.int32, (8, w2), 0) * blk
    own_a = st_ref[2 * me_i]
    own_b = st_ref[2 * me_i + 1]
    for i in range(R):
        ra = rk_ref[0, i, 0, own_a]
        rb = rk_ref[0, i, 0, own_b]
        for c in range(2):
            vp[0, c, i * rank:(i + 1) * rank, :] = packed(
                v_ref[0, i, 0, 0, c], v_ref[0, i, 0, 1, c], ra, rb
            )
        mk[0, i * 8:(i + 1) * 8, :] = (level < ra).astype(F32)

    pl.semaphore_wait(barrier, R * S - 1)

    pending = []

    def send(src, dst, ss, rs, i, c):
        copy = pltpu.make_async_remote_copy(
            src_ref=src, dst_ref=dst, send_sem=ss, recv_sem=rs,
            device_id={"rtile": i, "stile": c}, device_id_type=MESH,
        )
        copy.start()
        pending.append(copy)
        return copy

    v_copies = {}
    for d in range(1, S):
        c = lax.rem(me_c + S - d, S)
        v_copies[d] = (
            send(vp.at[0], vp.at[d], v_send.at[d], v_recv.at[d], me_i, c),
            send(mk.at[0], mk.at[d], m_send.at[d], m_recv.at[d], me_i, c),
        )

    for q in range(2):
        xs[q] = jnp.concatenate([x_ref[0, q, 0], x_ref[0, q, 1]], axis=1)

    lane = lax.broadcasted_iota(jnp.int32, (1, w2), 1)
    sgn = jnp.where(lane < w, 1.0, -1.0).astype(F32)

    cell = lax.broadcasted_iota(jnp.int32, (tile, w2), 0)
    ca = cell // EDGE
    cb = cell % EDGE
    has_e = (cb < EDGE - 1).astype(F32)
    has_w = (cb > 0).astype(F32)
    has_s = (ca < EDGE - 1).astype(F32)
    has_n = (ca > 0).astype(F32)

    def one_hot(shape, edge_dim):
        e = lax.broadcasted_iota(jnp.int32, shape, edge_dim)
        at = lax.broadcasted_iota(jnp.int32, shape, 1 - edge_dim)
        side = e // EDGE
        j = e % EDGE
        want = jnp.where(
            side == 0, j * EDGE + EDGE - 1,
            jnp.where(side == 1, (EDGE - 1) * EDGE + j, jnp.where(side == 2, j * EDGE, j)),
        )
        return (at == want).astype(F32).astype(BF16)

    take_edges = one_hot((4 * EDGE, tile), 0)
    put_edges = one_hot((tile, 4 * EDGE), 1)

    def mask_of(d):
        m = mk[d]
        return jnp.broadcast_to(m[:, None, :], (R * 8, blk, w2)).reshape(R * rank, w2) > 0.5

    for t in range(ITERS):
        edge_in = (edge_in0, edge_in1)[t]
        x0 = xs[0]
        x1 = xs[1]
        rhs_r = jnp.concatenate([x0, x1], axis=1).astype(BF16)
        rhs_i = jnp.concatenate([swap(x0) * sgn, swap(x1) * sgn], axis=1).astype(BF16)

        p_copies = []
        for d in range(S):
            if t == 0 and d:
                for copy in v_copies[d]:
                    copy.wait_recv()
            both = dot(vp[d, 0], rhs_r) + dot(vp[d, 1], rhs_i)
            pan = jnp.where(mask_of(d), both[:, :w2], both[:, w2:]).astype(BF16)
            pan_out[t, d] = pan.reshape(R, rank, w2)
            for k in reversed(range(R)):
                if d or k:
                    i = lax.rem(me_i + k, R)
                    p_copies.append(send(
                        pan_out.at[t, d, i], pan_in.at[t, d, me_i],
                        p_send.at[t, d, k], p_recv.at[t, d, k],
                        i, lax.rem(me_c + d, S),
                    ))
        pan_in[t, 0, me_i] = pan_out[t, 0, me_i]

        edges = dot(take_edges, rhs_r).astype(BF16)
        for q in range(2):
            edge_out[t, q] = edges[:, q * w2:(q + 1) * w2]
            edge_in[2 * me_i + q] = edges[:, q * w2:(q + 1) * w2]
        e_copies = []
        for k in range(1, R):
            e_copies.append(send(
                edge_out.at[t], edge_in.at[pl.ds(2 * me_i, 2)],
                e_send.at[t, k], e_recv.at[t, k], lax.rem(me_i + k, R), me_c,
            ))

        if t == 0:
            for p in range(R):
                ta = st_ref[2 * p]
                tb = st_ref[2 * p + 1]
                ra = rk_ref[0, me_i, 0, ta]
                rb = rk_ref[0, me_i, 0, tb]
                for c in range(2):
                    up[c, p * rank:(p + 1) * rank, :] = packed(
                        u_ref[0, 0, 0, ta, c], u_ref[0, 0, 0, tb, c], ra, rb
                    )
            for s in range(S):
                dl[s] = jnp.concatenate(
                    [d_ref[0, 0, 0, 0, :, s * w:(s + 1) * w], d_ref[0, 0, 0, 1, :, s * w:(s + 1) * w]],
                    axis=1,
                )

        for copy in p_copies:
            copy.wait_recv()
        b_copies = []
        for e in range(S):
            pan = pan_in[t, e].reshape(R * rank, w2)
            turned = (swap(pan.astype(F32)) * (-sgn)).astype(BF16)
            image = dot_t(up[0], pan) + dot_t(up[1], turned)
            misfit = image - dl[lax.rem(me_c + S - e, S)]
            mis_r = misfit.astype(BF16)
            mis_i = (swap(misfit) * sgn).astype(BF16)
            back = (dot(up[0], mis_r) + dot(up[1], mis_i)).astype(BF16)
            back_out[t, e] = back.reshape(R, rank, w2)
            for k in reversed(range(R)):
                if e or k:
                    q = lax.rem(me_i + k, R)
                    b_copies.append(send(
                        back_out.at[t, e, q], back_in.at[t, e, me_i],
                        b_send.at[t, e, k], b_recv.at[t, e, k],
                        q, lax.rem(me_c + S - e, S),
                    ))
        back_in[t, 0, me_i] = back_out[t, 0, me_i]

        for copy in e_copies:
            copy.wait_recv()
        ghosts = []
        degs = []
        for q in range(2):
            mine = st_ref[2 * me_i + q]
            parts = []
            deg = has_e + has_w + has_s + has_n
            for side in range(4):
                listed = nb_ref[mine, side]
                present = jnp.where(listed >= 0, 1.0, 0.0).astype(F32)
                want = jnp.maximum(listed, 0)
                slot = jnp.int32(0)
                for j in range(count):
                    slot = jnp.where(st_ref[j] == want, j, slot)
                opp = (side + 2) % 4
                ghost = edge_in[slot, opp * EDGE:(opp + 1) * EDGE, :].astype(F32)
                parts.append(ghost * present)
                border = (has_e, has_s, has_w, has_n)[side]
                deg = deg + (1.0 - border) * present
            ghosts.append(jnp.concatenate(parts, axis=0))
            degs.append(deg)
        ghost_sum = dot(put_edges, jnp.concatenate(ghosts, axis=1).astype(BF16))
        drift = []
        for q in range(2):
            x = xs[q]
            lap = (
                shift(x, -1) * has_e + shift(x, 1) * has_w
                + shift(x, -EDGE) * has_s + shift(x, EDGE) * has_n
                + ghost_sum[:, q * w2:(q + 1) * w2] - degs[q] * x
            )
            term = -0.25 * lap
            if t:
                term = term + (x - zs[q] + us[q])
            drift.append(term)

        for copy in b_copies:
            copy.wait_recv()
        grad = jnp.zeros((tile, 2 * w2), F32)
        for d in range(S):
            b = back_in[t, d].reshape(R * rank, w2).astype(F32)
            turned = swap(b) * (-sgn)
            m = mask_of(d)
            g_r = jnp.concatenate([jnp.where(m, b, 0.0), jnp.where(m, 0.0, b)], axis=1).astype(BF16)
            g_i = jnp.concatenate([jnp.where(m, turned, 0.0), jnp.where(m, 0.0, turned)], axis=1).astype(BF16)
            grad = grad + dot_t(vp[d, 0], g_r) + dot_t(vp[d, 1], g_i)

        for q in range(2):
            x = xs[q] - 0.1 * (grad[:, q * w2:(q + 1) * w2] + drift[q])
            summed = x + us[q] if t else x
            sq = summed * summed
            modulus = jnp.sqrt(sq + swap(sq))
            z = summed * (1.0 - 0.5 / jnp.maximum(modulus, 0.5))
            if t < ITERS - 1:
                xs[q] = x
                zs[q] = z
                us[q] = summed - z
            else:
                for c in range(2):
                    xo_ref[0, q, c] = x[:, c * w:(c + 1) * w]
                    zo_ref[0, q, c] = z[:, c * w:(c + 1) * w]

    for copy in pending:
        copy.wait_send()


def on_device(R, S, x_start, data, u_fac, v_fac, ranks, slot_tile, neighbours):
    w2 = 2 * x_start.shape[-1]
    tile = x_start.shape[-2]
    rank = v_fac.shape[-2]
    slots = x_start.shape[1]
    T = ITERS
    vmem = pl.BlockSpec(memory_space=pltpu.VMEM)
    smem = pl.BlockSpec(memory_space=pltpu.SMEM)
    out = jax.ShapeDtypeStruct(x_start.shape, F32)
    dma = pltpu.SemaphoreType.DMA
    return pl.pallas_call(
        functools.partial(kernel, R, S),
        out_shape=(out, out),
        in_specs=[vmem, vmem, vmem, vmem, smem, smem, smem],
        out_specs=(vmem, vmem),
        scratch_shapes=[
            pltpu.VMEM((S, 2, R * rank, tile), BF16),
            pltpu.VMEM((S, R * 8, w2), F32),
            pltpu.VMEM((2, R * rank, tile), BF16),
            pltpu.VMEM((S, tile, w2), F32),
            pltpu.VMEM((slots, tile, w2), F32),
            pltpu.VMEM((slots, tile, w2), F32),
            pltpu.VMEM((slots, tile, w2), F32),
            pltpu.VMEM((T, S, R, rank, w2), BF16),
            pltpu.VMEM((T, S, R, rank, w2), BF16),
            pltpu.VMEM((T, S, R, rank, w2), BF16),
            pltpu.VMEM((T, S, R, rank, w2), BF16),
            pltpu.VMEM((T, slots, 4 * EDGE, w2), BF16),
            pltpu.VMEM((slots * R, 4 * EDGE, w2), BF16),
            pltpu.VMEM((slots * R, 4 * EDGE, w2), BF16),
            dma((S,)), dma((S,)), dma((S,)), dma((S,)),
            dma((T, S, R)), dma((T, S, R)), dma((T, S, R)), dma((T, S, R)),
            dma((T, R)), dma((T, R)),
        ],
        compiler_params=pltpu.CompilerParams(
            collective_id=0, has_side_effects=True, vmem_limit_bytes=56 * 1024 * 1024
        ),
    )(x_start, data, u_fac, v_fac, ranks, slot_tile, neighbours)


def solution(mesh):
    in_specs = (
        P(("band", "freq"), "rtile", None, None, "stile"),
        P(("band", "freq"), "rtile", "stile", None, None, None),
        P(("band", "freq"), "rtile", "stile", None, None, None, None),
        P(("band", "freq"), None, "stile", "rtile", None, None, None),
        P(("band", "freq"), None, "stile", None),
        P(),
        P(),
    )
    out_specs = (
        P(("band", "freq"), "rtile", None, None, "stile"),
        P(("band", "freq"), "rtile", None, None, "stile"),
    )
    return jax.shard_map(
        functools.partial(on_device, mesh.shape["rtile"], mesh.shape["stile"]),
        mesh=mesh, in_specs=in_specs, out_specs=out_specs, check_vma=False,
    )
```

```python
import functools

import jax
import jax.numpy as jnp
from jax import lax
from jax.experimental import pallas as pl
from jax.experimental.pallas import tpu as pltpu
from jax.sharding import PartitionSpec as P

EDGE = 16
ITERS = 2
F32 = jnp.float32
BF16 = jnp.bfloat16
MESH = pl.DeviceIdType.MESH


def dot(a, b):
    return lax.dot_general(a, b, (((1,), (0,)), ((), ())), preferred_element_type=F32)


def dot_t(a, b):
    return lax.dot_general(a, b, (((0,), (0,)), ((), ())), preferred_element_type=F32)


def swap(v):
    w = v.shape[1] // 2
    if v.shape[1] == 128:
        return pltpu.roll(v, w, 1)
    return jnp.concatenate([v[:, w:], v[:, :w]], axis=1)


def shift(v, by):
    n = v.shape[0]
    return pltpu.roll(v, by % n, 0)


def kernel(
    R, S,
    x_ref, d_ref, u_ref, v_ref, rk_ref, st_ref, nb_ref,
    xo_ref, zo_ref,
    xv, dv, uv, vv, vp, mk, up, dl, xs, zs, us, xb,
    pan_out, pan_in, back_out, back_in, edge_out, edge_in0, edge_in1,
    in_sem, x_send, x_recv, v_send, v_recv, m_send, m_recv, p_send, p_recv, b_send, b_recv, e_send, e_recv,
):
    me_i = lax.axis_index("rtile")
    me_c = lax.axis_index("stile")
    rank = v_ref.shape[-2]
    tile = v_ref.shape[-1]
    w = x_ref.shape[-2]
    w2 = 2 * w
    count = st_ref.shape[0]
    blk = rank // 8

    barrier = pltpu.get_barrier_semaphore()
    for d in range(S):
        for k in range(R):
            if d or k:
                pl.semaphore_signal(
                    barrier, inc=1,
                    device_id={"rtile": lax.rem(me_i + k, R), "stile": lax.rem(me_c + d, S)},
                    device_id_type=MESH,
                )

    loads = [
        pltpu.make_async_copy(src, dst, in_sem.at[j])
        for j, (src, dst) in enumerate(((x_ref, xv), (v_ref, vv), (u_ref, uv), (d_ref, dv)))
    ]
    for load in loads:
        load.start()
    load_x, load_v, load_u, load_d = loads

    row = lax.broadcasted_iota(jnp.int32, (rank, tile), 0)

    def packed(a, b, ra, rb):
        a = a.astype(F32)
        b = b.astype(F32)
        b = jnp.concatenate([b[j * blk:(j + 1) * blk] for j in reversed(range(8))], axis=0)
        return jnp.where(row < ra, a, jnp.where(row >= rank - rb, b, 0.0)).astype(BF16)

    pending = []

    def send(src, dst, ss, rs, i, c):
        copy = pltpu.make_async_remote_copy(
            src_ref=src, dst_ref=dst, send_sem=ss, recv_sem=rs,
            device_id={"rtile": i, "stile": c}, device_id_type=MESH,
        )
        copy.start()
        pending.append(copy)
        return copy

    def one_hot(shape, edge_dim):
        e = lax.broadcasted_iota(jnp.int32, shape, edge_dim)
        at = lax.broadcasted_iota(jnp.int32, shape, 1 - edge_dim)
        side = e // EDGE
        j = e % EDGE
        want = jnp.where(
            side == 0, j * EDGE + EDGE - 1,
            jnp.where(side == 1, (EDGE - 1) * EDGE + j, jnp.where(side == 2, j * EDGE, j)),
        )
        return (at == want).astype(F32).astype(BF16)

    take_edges = one_hot((4 * EDGE, tile), 0)
    put_edges = one_hot((tile, 4 * EDGE), 1)
    lane = lax.broadcasted_iota(jnp.int32, (1, w2), 1)
    sgn = jnp.where(lane < w, 1.0, -1.0).astype(F32)

    def turned_field(v):
        return jnp.concatenate(
            [(swap(v[:, q * w2:(q + 1) * w2].astype(F32)) * sgn).astype(BF16) for q in range(2)], axis=1
        )

    def send_edges(t, edge_in, rhs_r):
        edges = dot(take_edges, rhs_r).astype(BF16)
        for q in range(2):
            edge_out[t, q] = edges[:, q * w2:(q + 1) * w2]
            edge_in[2 * me_i + q] = edges[:, q * w2:(q + 1) * w2]
        return [
            send(
                edge_out.at[t], edge_in.at[pl.ds(2 * me_i, 2)],
                e_send.at[t, k], e_recv.at[t, k], lax.rem(me_i + k, R), me_c,
            )
            for k in range(1, R)
        ]

    load_x.wait()
    for q in range(2):
        xs[q] = jnp.concatenate([xv[0, q, 0], xv[0, q, 1]], axis=0).T
        xb[0, :, q * w2:(q + 1) * w2] = xs[q].astype(BF16)

    pl.semaphore_wait(barrier, R * S - 1)

    x_copies = {
        e: send(xb.at[0], xb.at[e], x_send.at[e], x_recv.at[e], me_i, lax.rem(me_c + e, S))
        for e in range(1, S)
    }

    level = lax.broadcasted_iota(jnp.int32, (8, w2), 0) * blk
    own_a = st_ref[2 * me_i]
    own_b = st_ref[2 * me_i + 1]
    load_v.wait()
    for i in range(R):
        ra = rk_ref[0, i, 0, own_a]
        rb = rk_ref[0, i, 0, own_b]
        for c in range(2):
            vp[0, c, i * rank:(i + 1) * rank, :] = packed(
                vv[0, i, 0, 0, c], vv[0, i, 0, 1, c], ra, rb
            )
        mk[0, i * 8:(i + 1) * 8, :] = (level < ra).astype(F32)

    v_copies = {}
    for d in range(1, S):
        c = lax.rem(me_c + S - d, S)
        v_copies[d] = (
            send(vp.at[0], vp.at[d], v_send.at[d], v_recv.at[d], me_i, c),
            send(mk.at[0], mk.at[d], m_send.at[d], m_recv.at[d], me_i, c),
        )

    cell = lax.broadcasted_iota(jnp.int32, (tile, w2), 0)
    ca = cell // EDGE
    cb = cell % EDGE
    has_e = (cb < EDGE - 1).astype(F32)
    has_w = (cb > 0).astype(F32)
    has_s = (ca < EDGE - 1).astype(F32)
    has_n = (ca > 0).astype(F32)

    def mask_of(d):
        m = mk[d]
        return jnp.broadcast_to(m[:, None, :], (R * 8, blk, w2)).reshape(R * rank, w2) > 0.5

    for t in range(ITERS):
        edge_in = (edge_in0, edge_in1)[t]
        p_copies = [[] for _ in range(S)]
        if t:
            rhs_r = jnp.concatenate([xs[0], xs[1]], axis=1).astype(BF16)
            rhs_i = turned_field(rhs_r)
        for d in range(S):
            v = 0 if t == 0 else d
            if t == 0:
                if d:
                    x_copies[d].wait_recv()
                rhs_r = xb[d]
                rhs_i = turned_field(rhs_r)
            both = dot(vp[v, 0], rhs_r) + dot(vp[v, 1], rhs_i)
            pan = jnp.where(mask_of(v), both[:, :w2], both[:, w2:]).astype(BF16)
            pan_out[t, d] = pan.reshape(R, rank, w2)
            to = me_c if t == 0 else lax.rem(me_c + d, S)
            for k in reversed(range(R)):
                if k or (t and d):
                    i = lax.rem(me_i + k, R)
                    p_copies[d].append(send(
                        pan_out.at[t, d, i], pan_in.at[t, d, me_i],
                        p_send.at[t, d, k], p_recv.at[t, d, k], i, to,
                    ))
            if t == 0 or d == 0:
                pan_in[t, d, me_i] = pan_out[t, d, me_i]
            if t == 0 and d == 0:
                e_copies = send_edges(t, edge_in, rhs_r)
        if t:
            e_copies = send_edges(t, edge_in, rhs_r)

        if t == 0:
            load_u.wait()
            load_d.wait()
            for p in range(R):
                ta = st_ref[2 * p]
                tb = st_ref[2 * p + 1]
                ra = rk_ref[0, me_i, 0, ta]
                rb = rk_ref[0, me_i, 0, tb]
                for c in range(2):
                    up[c, p * rank:(p + 1) * rank, :] = packed(
                        uv[0, 0, 0, ta, c], uv[0, 0, 0, tb, c], ra, rb
                    )
            for s in range(S):
                dl[s] = jnp.concatenate(
                    [dv[0, 0, 0, 0, :, s * w:(s + 1) * w], dv[0, 0, 0, 1, :, s * w:(s + 1) * w]],
                    axis=1,
                )

        b_copies = [[] for _ in range(S)]
        for e in range(S):
            for copy in p_copies[e]:
                copy.wait_recv()
            pan = pan_in[t, e].reshape(R * rank, w2)
            turned = (swap(pan.astype(F32)) * (-sgn)).astype(BF16)
            image = dot_t(up[0], pan) + dot_t(up[1], turned)
            misfit = image - dl[lax.rem(me_c + S - e, S)]
            mis_r = misfit.astype(BF16)
            mis_i = (swap(misfit) * sgn).astype(BF16)
            back = (dot(up[0], mis_r) + dot(up[1], mis_i)).astype(BF16)
            back_out[t, e] = back.reshape(R, rank, w2)
            for k in reversed(range(R)):
                if e or k:
                    q = lax.rem(me_i + k, R)
                    b_copies[e].append(send(
                        back_out.at[t, e, q], back_in.at[t, e, me_i],
                        b_send.at[t, e, k], b_recv.at[t, e, k],
                        q, lax.rem(me_c + S - e, S),
                    ))
        back_in[t, 0, me_i] = back_out[t, 0, me_i]

        for copy in e_copies:
            copy.wait_recv()
        ghosts = []
        degs = []
        for q in range(2):
            mine = st_ref[2 * me_i + q]
            parts = []
            deg = has_e + has_w + has_s + has_n
            for side in range(4):
                listed = nb_ref[side, mine]
                present = jnp.where(listed >= 0, 1.0, 0.0).astype(F32)
                want = jnp.maximum(listed, 0)
                slot = jnp.int32(0)
                for j in range(count):
                    slot = jnp.where(st_ref[j] == want, j, slot)
                opp = (side + 2) % 4
                ghost = edge_in[slot, opp * EDGE:(opp + 1) * EDGE, :].astype(F32)
                parts.append(ghost * present)
                border = (has_e, has_s, has_w, has_n)[side]
                deg = deg + (1.0 - border) * present
            ghosts.append(jnp.concatenate(parts, axis=0))
            degs.append(deg)
        ghost_sum = dot(put_edges, jnp.concatenate(ghosts, axis=1).astype(BF16))
        drift = []
        for q in range(2):
            x = xs[q]
            lap = (
                shift(x, -1) * has_e + shift(x, 1) * has_w
                + shift(x, -EDGE) * has_s + shift(x, EDGE) * has_n
                + ghost_sum[:, q * w2:(q + 1) * w2] - degs[q] * x
            )
            term = -0.25 * lap
            if t:
                term = term + (x - zs[q] + us[q])
            drift.append(term)

        grad = jnp.zeros((tile, 2 * w2), F32)
        for d in range(S):
            if t == 0 and d:
                for copy in v_copies[d]:
                    copy.wait_recv()
            for copy in b_copies[d]:
                copy.wait_recv()
            b = back_in[t, d].reshape(R * rank, w2).astype(F32)
            turned = swap(b) * (-sgn)
            m = mask_of(d)
            g_r = jnp.concatenate([jnp.where(m, b, 0.0), jnp.where(m, 0.0, b)], axis=1).astype(BF16)
            g_i = jnp.concatenate([jnp.where(m, turned, 0.0), jnp.where(m, 0.0, turned)], axis=1).astype(BF16)
            grad = grad + dot_t(vp[d, 0], g_r) + dot_t(vp[d, 1], g_i)

        for q in range(2):
            x = xs[q] - 0.1 * (grad[:, q * w2:(q + 1) * w2] + drift[q])
            summed = x + us[q] if t else x
            sq = summed * summed
            modulus = jnp.sqrt(sq + swap(sq))
            z = summed * (1.0 - 0.5 / jnp.maximum(modulus, 0.5))
            if t < ITERS - 1:
                xs[q] = x
                zs[q] = z
                us[q] = summed - z
            else:
                xt = x.T
                zt = z.T
                for c in range(2):
                    xo_ref[0, q, c] = xt[c * w:(c + 1) * w]
                    zo_ref[0, q, c] = zt[c * w:(c + 1) * w]

    for copy in pending:
        copy.wait_send()


def on_device(R, S, x_start, data, u_fac, v_fac, ranks, slot_tile, neighbours):
    x_cells = jnp.swapaxes(x_start, -1, -2)
    w2 = 2 * x_start.shape[-1]
    tile = x_start.shape[-2]
    rank = v_fac.shape[-2]
    slots = x_start.shape[1]
    T = ITERS
    vmem = pl.BlockSpec(memory_space=pltpu.VMEM)
    smem = pl.BlockSpec(memory_space=pltpu.SMEM)
    hbm = pl.BlockSpec(memory_space=pl.ANY)
    out = jax.ShapeDtypeStruct(x_cells.shape, F32)
    dma = pltpu.SemaphoreType.DMA
    x_out, z_out = pl.pallas_call(
        functools.partial(kernel, R, S),
        out_shape=(out, out),
        in_specs=[hbm, hbm, hbm, hbm, smem, smem, smem],
        out_specs=(vmem, vmem),
        scratch_shapes=[
            pltpu.VMEM(x_cells.shape, F32),
            pltpu.VMEM(data.shape, F32),
            pltpu.VMEM(u_fac.shape, BF16),
            pltpu.VMEM(v_fac.shape, BF16),
            pltpu.VMEM((S, 2, R * rank, tile), BF16),
            pltpu.VMEM((S, R * 8, w2), F32),
            pltpu.VMEM((2, R * rank, tile), BF16),
            pltpu.VMEM((S, tile, w2), F32),
            pltpu.VMEM((slots, tile, w2), F32),
            pltpu.VMEM((slots, tile, w2), F32),
            pltpu.VMEM((slots, tile, w2), F32),
            pltpu.VMEM((S, tile, slots * w2), BF16),
            pltpu.VMEM((T, S, R, rank, w2), BF16),
            pltpu.VMEM((T, S, R, rank, w2), BF16),
            pltpu.VMEM((T, S, R, rank, w2), BF16),
            pltpu.VMEM((T, S, R, rank, w2), BF16),
            pltpu.VMEM((T, slots, 4 * EDGE, w2), BF16),
            pltpu.VMEM((slots * R, 4 * EDGE, w2), BF16),
            pltpu.VMEM((slots * R, 4 * EDGE, w2), BF16),
            dma((4,)), dma((S,)), dma((S,)),
            dma((S,)), dma((S,)), dma((S,)), dma((S,)),
            dma((T, S, R)), dma((T, S, R)), dma((T, S, R)), dma((T, S, R)),
            dma((T, R)), dma((T, R)),
        ],
        compiler_params=pltpu.CompilerParams(
            collective_id=0, has_side_effects=True, vmem_limit_bytes=56 * 1024 * 1024
        ),
    )(x_cells, data, u_fac, v_fac, ranks, slot_tile, neighbours.T)
    return jnp.swapaxes(x_out, -1, -2), jnp.swapaxes(z_out, -1, -2)


def solution(mesh):
    in_specs = (
        P(("band", "freq"), "rtile", None, None, "stile"),
        P(("band", "freq"), "rtile", "stile", None, None, None),
        P(("band", "freq"), "rtile", "stile", None, None, None, None),
        P(("band", "freq"), None, "stile", "rtile", None, None, None),
        P(("band", "freq"), None, "stile", None),
        P(),
        P(),
    )
    out_specs = (
        P(("band", "freq"), "rtile", None, None, "stile"),
        P(("band", "freq"), "rtile", None, None, "stile"),
    )
    return jax.shard_map(
        functools.partial(on_device, mesh.shape["rtile"], mesh.shape["stile"]),
        mesh=mesh, in_specs=in_specs, out_specs=out_specs, check_vma=False,
    )
```

```python
import functools

import jax
import jax.numpy as jnp
from jax import lax
from jax.experimental import pallas as pl
from jax.experimental.pallas import tpu as pltpu
from jax.sharding import PartitionSpec as P

EDGE = 16
ITERS = 2
F32 = jnp.float32
BF16 = jnp.bfloat16
MESH = pl.DeviceIdType.MESH


def dot(a, b):
    return lax.dot_general(a, b, (((1,), (0,)), ((), ())), preferred_element_type=F32)


def dot_t(a, b):
    return lax.dot_general(a, b, (((0,), (0,)), ((), ())), preferred_element_type=F32)


def swap(v):
    w = v.shape[1] // 2
    if v.shape[1] == 128:
        return pltpu.roll(v, w, 1)
    return jnp.concatenate([v[:, w:], v[:, :w]], axis=1)


def shift(v, by):
    n = v.shape[0]
    return pltpu.roll(v, by % n, 0)


def kernel(
    R, S,
    x_ref, d_ref, u_ref, v_ref, rk_ref, st_ref, nb_ref,
    xo_ref,
    xv, dv, uv, vv, vp, mk, up, dl, xs, zs, us, xb,
    pan_out, pan_in, back_out, back_in, edge_out, edge_in0, edge_in1,
    in_sem, x_send, x_recv, v_send, v_recv, m_send, m_recv, p_send, p_recv, b_send, b_recv, e_send, e_recv,
):
    me_i = lax.axis_index("rtile")
    me_c = lax.axis_index("stile")
    rank = v_ref.shape[-2]
    tile = v_ref.shape[-1]
    w = x_ref.shape[-2]
    w2 = 2 * w
    count = st_ref.shape[0]
    blk = rank // 8

    barrier = pltpu.get_barrier_semaphore()
    for d in range(S):
        for k in range(R):
            if d or k:
                pl.semaphore_signal(
                    barrier, inc=1,
                    device_id={"rtile": lax.rem(me_i + k, R), "stile": lax.rem(me_c + d, S)},
                    device_id_type=MESH,
                )

    loads = [
        pltpu.make_async_copy(src, dst, in_sem.at[j])
        for j, (src, dst) in enumerate(((x_ref, xv), (v_ref, vv), (u_ref, uv), (d_ref, dv)))
    ]
    for load in loads:
        load.start()
    load_x, load_v, load_u, load_d = loads

    row = lax.broadcasted_iota(jnp.int32, (rank, tile), 0)

    def packed(a, b, ra, rb):
        a = a.astype(F32)
        b = b.astype(F32)
        b = jnp.concatenate([b[j * blk:(j + 1) * blk] for j in reversed(range(8))], axis=0)
        return jnp.where(row < ra, a, jnp.where(row >= rank - rb, b, 0.0)).astype(BF16)

    pending = []

    def send(src, dst, ss, rs, i, c):
        copy = pltpu.make_async_remote_copy(
            src_ref=src, dst_ref=dst, send_sem=ss, recv_sem=rs,
            device_id={"rtile": i, "stile": c}, device_id_type=MESH,
        )
        copy.start()
        pending.append(copy)
        return copy

    def one_hot(shape, edge_dim):
        e = lax.broadcasted_iota(jnp.int32, shape, edge_dim)
        at = lax.broadcasted_iota(jnp.int32, shape, 1 - edge_dim)
        side = e // EDGE
        j = e % EDGE
        want = jnp.where(
            side == 0, j * EDGE + EDGE - 1,
            jnp.where(side == 1, (EDGE - 1) * EDGE + j, jnp.where(side == 2, j * EDGE, j)),
        )
        return (at == want).astype(F32).astype(BF16)

    take_edges = one_hot((4 * EDGE, tile), 0)
    put_edges = one_hot((tile, 4 * EDGE), 1)
    lane = lax.broadcasted_iota(jnp.int32, (1, w2), 1)
    sgn = jnp.where(lane < w, 1.0, -1.0).astype(F32)

    def turned_field(v):
        return jnp.concatenate(
            [(swap(v[:, q * w2:(q + 1) * w2].astype(F32)) * sgn).astype(BF16) for q in range(2)], axis=1
        )

    def send_edges(t, edge_in, rhs_r):
        edges = dot(take_edges, rhs_r).astype(BF16)
        for q in range(2):
            edge_out[t, q] = edges[:, q * w2:(q + 1) * w2]
            edge_in[2 * me_i + q] = edges[:, q * w2:(q + 1) * w2]
        return [
            send(
                edge_out.at[t], edge_in.at[pl.ds(2 * me_i, 2)],
                e_send.at[t, k], e_recv.at[t, k], lax.rem(me_i + k, R), me_c,
            )
            for k in range(1, R)
        ]

    load_x.wait()
    for q in range(2):
        xs[q] = jnp.concatenate([xv[0, q, 0], xv[0, q, 1]], axis=0).T
        xb[0, :, q * w2:(q + 1) * w2] = xs[q].astype(BF16)

    pl.semaphore_wait(barrier, R * S - 1)

    x_copies = {
        e: send(xb.at[0], xb.at[e], x_send.at[e], x_recv.at[e], me_i, lax.rem(me_c + e, S))
        for e in range(1, S)
    }

    level = lax.broadcasted_iota(jnp.int32, (8, w2), 0) * blk
    own_a = st_ref[2 * me_i]
    own_b = st_ref[2 * me_i + 1]
    load_v.wait()
    for i in range(R):
        ra = rk_ref[0, i, 0, own_a]
        rb = rk_ref[0, i, 0, own_b]
        for c in range(2):
            vp[0, c, i * rank:(i + 1) * rank, :] = packed(
                vv[0, i, 0, 0, c], vv[0, i, 0, 1, c], ra, rb
            )
        mk[0, i * 8:(i + 1) * 8, :] = (level < ra).astype(F32)

    cell = lax.broadcasted_iota(jnp.int32, (tile, w2), 0)
    ca = cell // EDGE
    cb = cell % EDGE
    has_e = (cb < EDGE - 1).astype(F32)
    has_w = (cb > 0).astype(F32)
    has_s = (ca < EDGE - 1).astype(F32)
    has_n = (ca > 0).astype(F32)

    def mask_of(d):
        m = mk[d]
        return jnp.broadcast_to(m[:, None, :], (R * 8, blk, w2)).reshape(R * rank, w2) > 0.5

    for t in range(ITERS):
        edge_in = (edge_in0, edge_in1)[t]
        p_copies = [[] for _ in range(S)]
        if t:
            rhs_r = jnp.concatenate([xs[0], xs[1]], axis=1).astype(BF16)
            rhs_i = turned_field(rhs_r)
        for d in range(S):
            v = 0 if t == 0 else d
            if t == 0:
                if d:
                    x_copies[d].wait_recv()
                rhs_r = xb[d]
                rhs_i = turned_field(rhs_r)
            both = dot(vp[v, 0], rhs_r) + dot(vp[v, 1], rhs_i)
            pan = jnp.where(mask_of(v), both[:, :w2], both[:, w2:]).astype(BF16)
            pan_out[t, d] = pan.reshape(R, rank, w2)
            to = me_c if t == 0 else lax.rem(me_c + d, S)
            for k in reversed(range(R)):
                if k or (t and d):
                    i = lax.rem(me_i + k, R)
                    p_copies[d].append(send(
                        pan_out.at[t, d, i], pan_in.at[t, d, me_i],
                        p_send.at[t, d, k], p_recv.at[t, d, k], i, to,
                    ))
            if t == 0 or d == 0:
                pan_in[t, d, me_i] = pan_out[t, d, me_i]
            if t == 0 and d == 0:
                e_copies = send_edges(t, edge_in, rhs_r)
        if t:
            e_copies = send_edges(t, edge_in, rhs_r)
        else:
            v_copies = {}
            for d in range(1, S):
                c = lax.rem(me_c + S - d, S)
                v_copies[d] = (
                    send(vp.at[0], vp.at[d], v_send.at[d], v_recv.at[d], me_i, c),
                    send(mk.at[0], mk.at[d], m_send.at[d], m_recv.at[d], me_i, c),
                )


        if t == 0:
            load_u.wait()
            load_d.wait()
            for p in range(R):
                ta = st_ref[2 * p]
                tb = st_ref[2 * p + 1]
                ra = rk_ref[0, me_i, 0, ta]
                rb = rk_ref[0, me_i, 0, tb]
                for c in range(2):
                    up[c, p * rank:(p + 1) * rank, :] = packed(
                        uv[0, 0, 0, ta, c], uv[0, 0, 0, tb, c], ra, rb
                    )
            for s in range(S):
                dl[s] = jnp.concatenate(
                    [dv[0, 0, 0, 0, :, s * w:(s + 1) * w], dv[0, 0, 0, 1, :, s * w:(s + 1) * w]],
                    axis=1,
                )

        b_copies = [[] for _ in range(S)]
        for e in range(S):
            for copy in p_copies[e]:
                copy.wait_recv()
            pan = pan_in[t, e].reshape(R * rank, w2)
            turned = (swap(pan.astype(F32)) * (-sgn)).astype(BF16)
            image = dot_t(up[0], pan) + dot_t(up[1], turned)
            misfit = image - dl[lax.rem(me_c + S - e, S)]
            mis_r = misfit.astype(BF16)
            mis_i = (swap(misfit) * sgn).astype(BF16)
            back = (dot(up[0], mis_r) + dot(up[1], mis_i)).astype(BF16)
            back_out[t, e] = back.reshape(R, rank, w2)
            for k in reversed(range(R)):
                if e or k:
                    q = lax.rem(me_i + k, R)
                    b_copies[e].append(send(
                        back_out.at[t, e, q], back_in.at[t, e, me_i],
                        b_send.at[t, e, k], b_recv.at[t, e, k],
                        q, lax.rem(me_c + S - e, S),
                    ))
        back_in[t, 0, me_i] = back_out[t, 0, me_i]

        for copy in e_copies:
            copy.wait_recv()
        ghosts = []
        degs = []
        for q in range(2):
            mine = st_ref[2 * me_i + q]
            parts = []
            deg = has_e + has_w + has_s + has_n
            for side in range(4):
                listed = nb_ref[side, mine]
                present = jnp.where(listed >= 0, 1.0, 0.0).astype(F32)
                want = jnp.maximum(listed, 0)
                slot = jnp.int32(0)
                for j in range(count):
                    slot = jnp.where(st_ref[j] == want, j, slot)
                opp = (side + 2) % 4
                ghost = edge_in[slot, opp * EDGE:(opp + 1) * EDGE, :].astype(F32)
                parts.append(ghost * present)
                border = (has_e, has_s, has_w, has_n)[side]
                deg = deg + (1.0 - border) * present
            ghosts.append(jnp.concatenate(parts, axis=0))
            degs.append(deg)
        ghost_sum = dot(put_edges, jnp.concatenate(ghosts, axis=1).astype(BF16))
        drift = []
        for q in range(2):
            x = xs[q]
            lap = (
                shift(x, -1) * has_e + shift(x, 1) * has_w
                + shift(x, -EDGE) * has_s + shift(x, EDGE) * has_n
                + ghost_sum[:, q * w2:(q + 1) * w2] - degs[q] * x
            )
            term = -0.25 * lap
            if t:
                term = term + (x - zs[q] + us[q])
            drift.append(term)

        grad = jnp.zeros((tile, 2 * w2), F32)
        for d in range(S):
            if t == 0 and d:
                for copy in v_copies[d]:
                    copy.wait_recv()
            for copy in b_copies[d]:
                copy.wait_recv()
            b = back_in[t, d].reshape(R * rank, w2).astype(F32)
            turned = swap(b) * (-sgn)
            m = mask_of(d)
            g_r = jnp.concatenate([jnp.where(m, b, 0.0), jnp.where(m, 0.0, b)], axis=1).astype(BF16)
            g_i = jnp.concatenate([jnp.where(m, turned, 0.0), jnp.where(m, 0.0, turned)], axis=1).astype(BF16)
            grad = grad + dot_t(vp[d, 0], g_r) + dot_t(vp[d, 1], g_i)

        for q in range(2):
            x = xs[q] - 0.1 * (grad[:, q * w2:(q + 1) * w2] + drift[q])
            summed = x + us[q] if t else x
            sq = summed * summed
            modulus = jnp.sqrt(sq + swap(sq))
            z = summed * (1.0 - 0.5 / jnp.maximum(modulus, 0.5))
            if t < ITERS - 1:
                xs[q] = x
                zs[q] = z
                us[q] = summed - z
            else:
                xt = x.T
                zt = z.T
                for c in range(2):
                    xo_ref[0, 0, q, c] = xt[c * w:(c + 1) * w]
                    xo_ref[1, 0, q, c] = zt[c * w:(c + 1) * w]

    for copy in pending:
        copy.wait_send()


def on_device(R, S, x_start, data, u_fac, v_fac, ranks, slot_tile, neighbours):
    x_cells = jnp.swapaxes(x_start, -1, -2)
    w2 = 2 * x_start.shape[-1]
    tile = x_start.shape[-2]
    rank = v_fac.shape[-2]
    slots = x_start.shape[1]
    T = ITERS
    vmem = pl.BlockSpec(memory_space=pltpu.VMEM)
    smem = pl.BlockSpec(memory_space=pltpu.SMEM)
    hbm = pl.BlockSpec(memory_space=pl.ANY)
    out = jax.ShapeDtypeStruct((2,) + x_cells.shape, F32)
    dma = pltpu.SemaphoreType.DMA
    both = pl.pallas_call(
        functools.partial(kernel, R, S),
        out_shape=out,
        in_specs=[hbm, hbm, hbm, hbm, smem, smem, smem],
        out_specs=vmem,
        scratch_shapes=[
            pltpu.VMEM(x_cells.shape, F32),
            pltpu.VMEM(data.shape, F32),
            pltpu.VMEM(u_fac.shape, BF16),
            pltpu.VMEM(v_fac.shape, BF16),
            pltpu.VMEM((S, 2, R * rank, tile), BF16),
            pltpu.VMEM((S, R * 8, w2), F32),
            pltpu.VMEM((2, R * rank, tile), BF16),
            pltpu.VMEM((S, tile, w2), F32),
            pltpu.VMEM((slots, tile, w2), F32),
            pltpu.VMEM((slots, tile, w2), F32),
            pltpu.VMEM((slots, tile, w2), F32),
            pltpu.VMEM((S, tile, slots * w2), BF16),
            pltpu.VMEM((T, S, R, rank, w2), BF16),
            pltpu.VMEM((T, S, R, rank, w2), BF16),
            pltpu.VMEM((T, S, R, rank, w2), BF16),
            pltpu.VMEM((T, S, R, rank, w2), BF16),
            pltpu.VMEM((T, slots, 4 * EDGE, w2), BF16),
            pltpu.VMEM((slots * R, 4 * EDGE, w2), BF16),
            pltpu.VMEM((slots * R, 4 * EDGE, w2), BF16),
            dma((4,)), dma((S,)), dma((S,)),
            dma((S,)), dma((S,)), dma((S,)), dma((S,)),
            dma((T, S, R)), dma((T, S, R)), dma((T, S, R)), dma((T, S, R)),
            dma((T, R)), dma((T, R)),
        ],
        compiler_params=pltpu.CompilerParams(
            collective_id=0, has_side_effects=True, vmem_limit_bytes=56 * 1024 * 1024
        ),
    )(x_cells, data, u_fac, v_fac, ranks, slot_tile, neighbours.T)
    return jnp.swapaxes(both[0], -1, -2), jnp.swapaxes(both[1], -1, -2)


def solution(mesh):
    in_specs = (
        P(("band", "freq"), "rtile", None, None, "stile"),
        P(("band", "freq"), "rtile", "stile", None, None, None),
        P(("band", "freq"), "rtile", "stile", None, None, None, None),
        P(("band", "freq"), None, "stile", "rtile", None, None, None),
        P(("band", "freq"), None, "stile", None),
        P(),
        P(),
    )
    out_specs = (
        P(("band", "freq"), "rtile", None, None, "stile"),
        P(("band", "freq"), "rtile", None, None, "stile"),
    )
    return jax.shard_map(
        functools.partial(on_device, mesh.shape["rtile"], mesh.shape["stile"]),
        mesh=mesh, in_specs=in_specs, out_specs=out_specs, check_vma=False,
    )
```

```python
import functools

import jax
import jax.numpy as jnp
from jax import lax
from jax.experimental import pallas as pl
from jax.experimental.pallas import tpu as pltpu
from jax.sharding import PartitionSpec as P

EDGE = 16
ITERS = 2
F32 = jnp.float32
BF16 = jnp.bfloat16
MESH = pl.DeviceIdType.MESH


def dot(a, b):
    return lax.dot_general(a, b, (((1,), (0,)), ((), ())), preferred_element_type=F32)


def dot_t(a, b):
    return lax.dot_general(a, b, (((0,), (0,)), ((), ())), preferred_element_type=F32)


def swap(v):
    w = v.shape[1] // 2
    if v.shape[1] == 128:
        return pltpu.roll(v, w, 1)
    return jnp.concatenate([v[:, w:], v[:, :w]], axis=1)


def shift(v, by):
    n = v.shape[0]
    return pltpu.roll(v, by % n, 0)


def kernel(
    R, S,
    x_ref, d_ref, u_ref, v_ref, rk_ref, st_ref, nb_ref,
    xo_ref,
    xv, dv, uv, vv, vp, mk, up, dl, xs, zs, us, xb,
    pan_out, pan_in, back_out, back_in, edge_out, edge_in0, edge_in1,
    ov, o_sem, in_sem, x_send, x_recv, v_send, v_recv, m_send, m_recv, p_send, p_recv, b_send, b_recv, e_send, e_recv,
):
    me_i = lax.axis_index("rtile")
    me_c = lax.axis_index("stile")
    rank = v_ref.shape[-2]
    tile = v_ref.shape[-1]
    w = x_ref.shape[-2]
    w2 = 2 * w
    count = st_ref.shape[0]
    blk = rank // 8

    barrier = pltpu.get_barrier_semaphore()
    for d in range(S):
        for k in range(R):
            if d or k:
                pl.semaphore_signal(
                    barrier, inc=1,
                    device_id={"rtile": lax.rem(me_i + k, R), "stile": lax.rem(me_c + d, S)},
                    device_id_type=MESH,
                )

    loads = [
        pltpu.make_async_copy(src, dst, in_sem.at[j])
        for j, (src, dst) in enumerate(((x_ref, xv), (v_ref, vv), (u_ref, uv), (d_ref, dv)))
    ]
    for load in loads:
        load.start()
    load_x, load_v, load_u, load_d = loads

    row = lax.broadcasted_iota(jnp.int32, (rank, tile), 0)

    def packed(a, b, ra, rb):
        a = a.astype(F32)
        b = b.astype(F32)
        b = jnp.concatenate([b[j * blk:(j + 1) * blk] for j in reversed(range(8))], axis=0)
        return jnp.where(row < ra, a, jnp.where(row >= rank - rb, b, 0.0)).astype(BF16)

    pending = []
    stores = []

    def send(src, dst, ss, rs, i, c):
        copy = pltpu.make_async_remote_copy(
            src_ref=src, dst_ref=dst, send_sem=ss, recv_sem=rs,
            device_id={"rtile": i, "stile": c}, device_id_type=MESH,
        )
        copy.start()
        pending.append(copy)
        return copy

    def one_hot(shape, edge_dim):
        e = lax.broadcasted_iota(jnp.int32, shape, edge_dim)
        at = lax.broadcasted_iota(jnp.int32, shape, 1 - edge_dim)
        side = e // EDGE
        j = e % EDGE
        want = jnp.where(
            side == 0, j * EDGE + EDGE - 1,
            jnp.where(side == 1, (EDGE - 1) * EDGE + j, jnp.where(side == 2, j * EDGE, j)),
        )
        return (at == want).astype(F32).astype(BF16)

    take_edges = one_hot((4 * EDGE, tile), 0)
    put_edges = one_hot((tile, 4 * EDGE), 1)
    lane = lax.broadcasted_iota(jnp.int32, (1, w2), 1)
    sgn = jnp.where(lane < w, 1.0, -1.0).astype(F32)

    def turned_field(v):
        return jnp.concatenate(
            [(swap(v[:, q * w2:(q + 1) * w2].astype(F32)) * sgn).astype(BF16) for q in range(2)], axis=1
        )

    def send_edges(t, edge_in, rhs_r):
        edges = dot(take_edges, rhs_r).astype(BF16)
        for q in range(2):
            edge_out[t, q] = edges[:, q * w2:(q + 1) * w2]
            edge_in[2 * me_i + q] = edges[:, q * w2:(q + 1) * w2]
        return [
            send(
                edge_out.at[t], edge_in.at[pl.ds(2 * me_i, 2)],
                e_send.at[t, k], e_recv.at[t, k], lax.rem(me_i + k, R), me_c,
            )
            for k in range(1, R)
        ]

    load_x.wait()
    for q in range(2):
        xs[q] = jnp.concatenate([xv[0, q, 0], xv[0, q, 1]], axis=0).T
        xb[0, :, q * w2:(q + 1) * w2] = xs[q].astype(BF16)

    pl.semaphore_wait(barrier, R * S - 1)

    x_copies = {
        e: send(xb.at[0], xb.at[e], x_send.at[e], x_recv.at[e], me_i, lax.rem(me_c + e, S))
        for e in range(1, S)
    }

    level = lax.broadcasted_iota(jnp.int32, (8, w2), 0) * blk
    own_a = st_ref[2 * me_i]
    own_b = st_ref[2 * me_i + 1]
    load_v.wait()
    for i in range(R):
        ra = rk_ref[0, i, 0, own_a]
        rb = rk_ref[0, i, 0, own_b]
        for c in range(2):
            vp[0, c, i * rank:(i + 1) * rank, :] = packed(
                vv[0, i, 0, 0, c], vv[0, i, 0, 1, c], ra, rb
            )
        mk[0, i * 8:(i + 1) * 8, :] = (level < ra).astype(F32)

    cell = lax.broadcasted_iota(jnp.int32, (tile, w2), 0)
    ca = cell // EDGE
    cb = cell % EDGE
    has_e = (cb < EDGE - 1).astype(F32)
    has_w = (cb > 0).astype(F32)
    has_s = (ca < EDGE - 1).astype(F32)
    has_n = (ca > 0).astype(F32)

    def mask_of(d):
        m = mk[d]
        return jnp.broadcast_to(m[:, None, :], (R * 8, blk, w2)).reshape(R * rank, w2) > 0.5

    for t in range(ITERS):
        edge_in = (edge_in0, edge_in1)[t]
        p_copies = [[] for _ in range(S)]
        if t:
            rhs_r = jnp.concatenate([xs[0], xs[1]], axis=1).astype(BF16)
            rhs_i = turned_field(rhs_r)
        for d in range(S):
            v = 0 if t == 0 else d
            if t == 0:
                if d:
                    x_copies[d].wait_recv()
                rhs_r = xb[d]
                rhs_i = turned_field(rhs_r)
            both = dot(vp[v, 0], rhs_r) + dot(vp[v, 1], rhs_i)
            pan = jnp.where(mask_of(v), both[:, :w2], both[:, w2:]).astype(BF16)
            pan_out[t, d] = pan.reshape(R, rank, w2)
            to = me_c if t == 0 else lax.rem(me_c + d, S)
            for k in reversed(range(R)):
                if k or (t and d):
                    i = lax.rem(me_i + k, R)
                    p_copies[d].append(send(
                        pan_out.at[t, d, i], pan_in.at[t, d, me_i],
                        p_send.at[t, d, k], p_recv.at[t, d, k], i, to,
                    ))
            if t == 0 or d == 0:
                pan_in[t, d, me_i] = pan_out[t, d, me_i]
            if t == 0 and d == 0:
                e_copies = send_edges(t, edge_in, rhs_r)
        if t:
            e_copies = send_edges(t, edge_in, rhs_r)
        else:
            v_copies = {}
            for d in range(1, S):
                c = lax.rem(me_c + S - d, S)
                v_copies[d] = (
                    send(vp.at[0], vp.at[d], v_send.at[d], v_recv.at[d], me_i, c),
                    send(mk.at[0], mk.at[d], m_send.at[d], m_recv.at[d], me_i, c),
                )


        if t == 0:
            load_u.wait()
            load_d.wait()
            for p in range(R):
                ta = st_ref[2 * p]
                tb = st_ref[2 * p + 1]
                ra = rk_ref[0, me_i, 0, ta]
                rb = rk_ref[0, me_i, 0, tb]
                for c in range(2):
                    up[c, p * rank:(p + 1) * rank, :] = packed(
                        uv[0, 0, 0, ta, c], uv[0, 0, 0, tb, c], ra, rb
                    )
            for s in range(S):
                dl[s] = jnp.concatenate(
                    [dv[0, 0, 0, 0, :, s * w:(s + 1) * w], dv[0, 0, 0, 1, :, s * w:(s + 1) * w]],
                    axis=1,
                )

        b_copies = [[] for _ in range(S)]
        for e in range(S):
            for copy in p_copies[e]:
                copy.wait_recv()
            pan = pan_in[t, e].reshape(R * rank, w2)
            turned = (swap(pan.astype(F32)) * (-sgn)).astype(BF16)
            image = dot_t(up[0], pan) + dot_t(up[1], turned)
            misfit = image - dl[lax.rem(me_c + S - e, S)]
            mis_r = misfit.astype(BF16)
            mis_i = (swap(misfit) * sgn).astype(BF16)
            back = (dot(up[0], mis_r) + dot(up[1], mis_i)).astype(BF16)
            back_out[t, e] = back.reshape(R, rank, w2)
            for k in reversed(range(R)):
                if e or k:
                    q = lax.rem(me_i + k, R)
                    b_copies[e].append(send(
                        back_out.at[t, e, q], back_in.at[t, e, me_i],
                        b_send.at[t, e, k], b_recv.at[t, e, k],
                        q, lax.rem(me_c + S - e, S),
                    ))
        back_in[t, 0, me_i] = back_out[t, 0, me_i]

        for copy in e_copies:
            copy.wait_recv()
        ghosts = []
        degs = []
        for q in range(2):
            mine = st_ref[2 * me_i + q]
            parts = []
            deg = has_e + has_w + has_s + has_n
            for side in range(4):
                listed = nb_ref[side, mine]
                present = jnp.where(listed >= 0, 1.0, 0.0).astype(F32)
                want = jnp.maximum(listed, 0)
                slot = jnp.int32(0)
                for j in range(count):
                    slot = jnp.where(st_ref[j] == want, j, slot)
                opp = (side + 2) % 4
                ghost = edge_in[slot, opp * EDGE:(opp + 1) * EDGE, :].astype(F32)
                parts.append(ghost * present)
                border = (has_e, has_s, has_w, has_n)[side]
                deg = deg + (1.0 - border) * present
            ghosts.append(jnp.concatenate(parts, axis=0))
            degs.append(deg)
        ghost_sum = dot(put_edges, jnp.concatenate(ghosts, axis=1).astype(BF16))
        drift = []
        for q in range(2):
            x = xs[q]
            lap = (
                shift(x, -1) * has_e + shift(x, 1) * has_w
                + shift(x, -EDGE) * has_s + shift(x, EDGE) * has_n
                + ghost_sum[:, q * w2:(q + 1) * w2] - degs[q] * x
            )
            term = -0.25 * lap
            if t:
                term = term + (x - zs[q] + us[q])
            drift.append(term)

        grad = jnp.zeros((tile, 2 * w2), F32)
        for d in range(S):
            if t == 0 and d:
                for copy in v_copies[d]:
                    copy.wait_recv()
            for copy in b_copies[d]:
                copy.wait_recv()
            b = back_in[t, d].reshape(R * rank, w2).astype(F32)
            turned = swap(b) * (-sgn)
            m = mask_of(d)
            g_r = jnp.concatenate([jnp.where(m, b, 0.0), jnp.where(m, 0.0, b)], axis=1).astype(BF16)
            g_i = jnp.concatenate([jnp.where(m, turned, 0.0), jnp.where(m, 0.0, turned)], axis=1).astype(BF16)
            grad = grad + dot_t(vp[d, 0], g_r) + dot_t(vp[d, 1], g_i)

        for q in range(2):
            x = xs[q] - 0.1 * (grad[:, q * w2:(q + 1) * w2] + drift[q])
            summed = x + us[q] if t else x
            sq = summed * summed
            modulus = jnp.sqrt(sq + swap(sq))
            z = summed * (1.0 - 0.5 / jnp.maximum(modulus, 0.5))
            if t < ITERS - 1:
                xs[q] = x
                zs[q] = z
                us[q] = summed - z
            else:
                xt = x.T
                zt = z.T
                for c in range(2):
                    ov[0, 0, q, c] = xt[c * w:(c + 1) * w]
                    ov[1, 0, q, c] = zt[c * w:(c + 1) * w]
                for j in range(2):
                    copy = pltpu.make_async_copy(ov.at[j, 0, q], xo_ref.at[j, 0, q], o_sem.at[j, q])
                    copy.start()
                    stores.append(copy)

    for copy in stores:
        copy.wait()
    for copy in pending:
        copy.wait_send()


def on_device(R, S, x_start, data, u_fac, v_fac, ranks, slot_tile, neighbours):
    x_cells = jnp.swapaxes(x_start, -1, -2)
    w2 = 2 * x_start.shape[-1]
    tile = x_start.shape[-2]
    rank = v_fac.shape[-2]
    slots = x_start.shape[1]
    T = ITERS
    vmem = pl.BlockSpec(memory_space=pltpu.VMEM)
    smem = pl.BlockSpec(memory_space=pltpu.SMEM)
    hbm = pl.BlockSpec(memory_space=pl.ANY)
    out = jax.ShapeDtypeStruct((2,) + x_cells.shape, F32)
    dma = pltpu.SemaphoreType.DMA
    both = pl.pallas_call(
        functools.partial(kernel, R, S),
        out_shape=out,
        in_specs=[hbm, hbm, hbm, hbm, smem, smem, smem],
        out_specs=hbm,
        scratch_shapes=[
            pltpu.VMEM(x_cells.shape, F32),
            pltpu.VMEM(data.shape, F32),
            pltpu.VMEM(u_fac.shape, BF16),
            pltpu.VMEM(v_fac.shape, BF16),
            pltpu.VMEM((S, 2, R * rank, tile), BF16),
            pltpu.VMEM((S, R * 8, w2), F32),
            pltpu.VMEM((2, R * rank, tile), BF16),
            pltpu.VMEM((S, tile, w2), F32),
            pltpu.VMEM((slots, tile, w2), F32),
            pltpu.VMEM((slots, tile, w2), F32),
            pltpu.VMEM((slots, tile, w2), F32),
            pltpu.VMEM((S, tile, slots * w2), BF16),
            pltpu.VMEM((T, S, R, rank, w2), BF16),
            pltpu.VMEM((T, S, R, rank, w2), BF16),
            pltpu.VMEM((T, S, R, rank, w2), BF16),
            pltpu.VMEM((T, S, R, rank, w2), BF16),
            pltpu.VMEM((T, slots, 4 * EDGE, w2), BF16),
            pltpu.VMEM((slots * R, 4 * EDGE, w2), BF16),
            pltpu.VMEM((slots * R, 4 * EDGE, w2), BF16),
            pltpu.VMEM((2,) + x_cells.shape, F32), dma((2, 2)),
            dma((4,)), dma((S,)), dma((S,)),
            dma((S,)), dma((S,)), dma((S,)), dma((S,)),
            dma((T, S, R)), dma((T, S, R)), dma((T, S, R)), dma((T, S, R)),
            dma((T, R)), dma((T, R)),
        ],
        compiler_params=pltpu.CompilerParams(
            collective_id=0, has_side_effects=True, vmem_limit_bytes=56 * 1024 * 1024
        ),
    )(x_cells, data, u_fac, v_fac, ranks, slot_tile, neighbours.T)
    return jnp.swapaxes(both[0], -1, -2), jnp.swapaxes(both[1], -1, -2)


def solution(mesh):
    in_specs = (
        P(("band", "freq"), "rtile", None, None, "stile"),
        P(("band", "freq"), "rtile", "stile", None, None, None),
        P(("band", "freq"), "rtile", "stile", None, None, None, None),
        P(("band", "freq"), None, "stile", "rtile", None, None, None),
        P(("band", "freq"), None, "stile", None),
        P(),
        P(),
    )
    out_specs = (
        P(("band", "freq"), "rtile", None, None, "stile"),
        P(("band", "freq"), "rtile", None, None, "stile"),
    )
    return jax.shard_map(
        functools.partial(on_device, mesh.shape["rtile"], mesh.shape["stile"]),
        mesh=mesh, in_specs=in_specs, out_specs=out_specs, check_vma=False,
    )
```
